128 devices in a mesh: dp: 32 (over x, z_lo, y), fsdp: 4 (over z_hi, core).
Axes of the slice: x: 4, y: 4, z: 4 (z_hi: 2, z_lo: 2; z = z_hi * 2 + z_lo), core: 2. Of those that a mesh axis runs over, the one named last changes fastest.
Arguments:
- image_feats: bfloat16 [16384, 1152], P('dp'), may hold values from -6 to 6
- text_feats: bfloat16 [16384, 1152], P(('dp', 'fsdp')), may hold values from -6 to 6
- w_image: bfloat16 [1152, 1152], P('fsdp'), may hold values from -0.1875 to 0.1875
- w_text: bfloat16 [1152, 1152], P('fsdp'), may hold values from -0.1875 to 0.1875
- logit_scale: float32 [1], replicated, may hold values from 1.6 to 3
- logit_bias: float32 [1], replicated, may hold values from -3 to -1
Outputs:
- loss_mean: float32 [1], replicated
- grad_w_image: float32 [1152, 1152], P('fsdp')
- grad_w_text: float32 [1152, 1152], P('fsdp')
- grad_scale: float32 [1], replicated
- grad_bias: float32 [1], replicated
The draws below stay inside these ranges and needn't reach their ends.
All inputs are finite; a program needn't handle non-finite values.
Results may differ from the reference program's by a relative error of at most 0.002.
Values may be sent and summed in bfloat16 or wider, within the bound.
A program may use at most 192 MiB of HBM per device.

```python
import jax
import jax.numpy as jnp
from jax import lax

D = 1152
E = 1152
TOK_DEV = 512
TOKENS = 16384


def steps_of(stream_key, extent, pieces, low, largest):
    loudness = 1.0
    for axis_at, shards_of in pieces:
        draws = jax.random.uniform(jax.random.fold_in(jax.random.fold_in(stream_key, 6), axis_at), (shards_of,), jnp.float32, low / len(pieces), largest / len(pieces))
        loudness = loudness * jnp.repeat(jnp.exp(draws), extent[axis_at] // shards_of).reshape((-1,) + (1,) * (len(extent) - 1 - axis_at))
    return loudness


def scatter_about(stream_key, shape, scale, bound, cuts=(), held_as=jnp.bfloat16):
    loudness = steps_of(stream_key, shape, cuts, -0.22, 0.18) if cuts else 1.0
    result = jax.random.normal(stream_key, shape, jnp.float32) * scale * loudness
    return jnp.minimum(jnp.maximum(result, -bound), bound).astype(held_as)


def setup_inputs(seed: int = 0) -> dict:
    key_list = jax.random.split(jax.random.key(seed), 7)
    image_feats = scatter_about(key_list[0], (TOKENS, D), 1.0, 6.0, ((0, 32),))
    text_feats = scatter_about(key_list[1], (TOKENS, D), 1.0, 6.0, ((0, 128),))
    w_image = scatter_about(key_list[2], (D, E), D ** -0.5, 0.1875, ((0, 4),))
    w_text = scatter_about(key_list[3], (D, E), D ** -0.5, 0.1875, ((0, 4),))
    logit_scale = jnp.clip(jax.random.uniform(key_list[4], (1,), jnp.float32, 1.6, 3.0), 1.6, 3.0)
    logit_bias = jnp.clip(jax.random.uniform(key_list[5], (1,), jnp.float32, -3.0, -1.0), -3.0, -1.0)
    return {"image_feats": image_feats, "text_feats": text_feats, "w_image": w_image, "w_text": w_text, "logit_scale": logit_scale, "logit_bias": logit_bias}


def unit_rows(proj):
    inverse = lax.rsqrt(lax.optimization_barrier(jnp.sum(proj * proj, axis=-1, keepdims=True)) + 1e-06)
    return (proj * inverse, inverse)

def back_unit(unit, inverse, grad):
    inner = lax.optimization_barrier(jnp.sum(unit * grad, axis=-1, keepdims=True))
    return (inverse * (grad - unit * inner)).astype(jnp.bfloat16)

def reference(image_feats, text_feats, w_image, w_text, logit_scale, logit_bias):
    img_proj = jnp.dot(image_feats, w_image, preferred_element_type=jnp.float32)
    txt_proj = jnp.dot(text_feats, w_text, preferred_element_type=jnp.float32)
    img_unit, img_inv = unit_rows(img_proj)
    txt_unit, txt_inv = unit_rows(txt_proj)
    img_emb = img_unit.astype(jnp.bfloat16)
    txt_emb = txt_unit.astype(jnp.bfloat16)
    temper = jnp.exp(logit_scale[0])
    offset = logit_bias[0]
    total = TOKENS
    columns = jnp.arange(total, dtype=jnp.int32)
    block_count = total // TOK_DEV

    def one_block(state, index):
        grad_txt, loss_sum, scale_sum, bias_sum = state
        first = (index * TOK_DEV).astype(jnp.int32)
        block_emb = lax.dynamic_slice_in_dim(img_emb, first, TOK_DEV, 0)
        cosines = jnp.dot(block_emb, txt_emb.T, preferred_element_type=jnp.float32)
        logits = temper * cosines + offset
        row_ids = first + jnp.arange(TOK_DEV, dtype=jnp.int32)
        labels = jnp.where(row_ids[:, None] == columns[None, :], 1.0, -1.0).astype(jnp.float32)
        loss_sum = loss_sum - jnp.sum(jax.nn.log_sigmoid(labels * logits))
        grad_logits = -labels * jax.nn.sigmoid(-labels * logits) / total
        scale_sum = scale_sum + temper * jnp.sum(grad_logits * cosines)
        bias_sum = bias_sum + jnp.sum(grad_logits)
        grad_low = grad_logits.astype(jnp.bfloat16)
        grad_img_block = temper * jnp.dot(grad_low, txt_emb, preferred_element_type=jnp.float32)
        grad_txt = grad_txt + temper * jnp.dot(grad_low.T, block_emb, preferred_element_type=jnp.float32)
        return ((grad_txt, loss_sum, scale_sum, bias_sum), grad_img_block)
    start_state = (jnp.zeros((total, E), jnp.float32), jnp.zeros((), jnp.float32), jnp.zeros((), jnp.float32), jnp.zeros((), jnp.float32))
    final_state, grad_blocks = lax.scan(one_block, start_state, jnp.arange(block_count, dtype=jnp.int32))
    grad_txt, loss_sum, scale_sum, bias_sum = final_state
    grad_img = grad_blocks.reshape(total, E)
    proj_grad_img = back_unit(img_unit, img_inv, grad_img)
    proj_grad_txt = back_unit(txt_unit, txt_inv, grad_txt)
    grad_w_image = jnp.dot(image_feats.T, proj_grad_img, preferred_element_type=jnp.float32)
    grad_w_text = jnp.dot(text_feats.T, proj_grad_txt, preferred_element_type=jnp.float32)
    loss_mean = (loss_sum / total / total).reshape(1)
    return (loss_mean, grad_w_image, grad_w_text, scale_sum.reshape(1), bias_sum.reshape(1))
```

```python
import functools

import jax
import jax.numpy as jnp
from jax import lax
from jax.experimental import pallas as pl
from jax.experimental.pallas import tpu as pltpu
from jax.sharding import PartitionSpec as P

MESH = pl.DeviceIdType.MESH
BF = jnp.bfloat16
F32 = jnp.float32
LAST = (((1,), (1,)), ((), ()))
FIRST = (((0,), (0,)), ((), ()))
LOG2E = 1.4426950408889634


class Links:
    def __init__(self, send_sems, recv_sems):
        self.send_sems, self.recv_sems, self.used, self.open = send_sems, recv_sems, 0, []

    def send(self, src, dst, device):
        copy = pltpu.make_async_remote_copy(
            src_ref=src,
            dst_ref=dst,
            send_sem=self.send_sems.at[self.used],
            recv_sem=self.recv_sems.at[self.used],
            device_id=device,
            device_id_type=MESH,
        )
        self.used += 1
        copy.start()
        self.open.append(copy)
        return copy

    def flush(self):
        for copy in self.open:
            copy.wait_send()
        self.open = []


class RingGather:
    def __init__(self, links, slots, cut, right, left):
        self.links, self.slots, self.right, self.left = links, slots, right, left

    def start(self):
        self.from_left = self.links.send(self.slots(0, None), self.slots(3, None), self.right)
        self.from_right = self.links.send(self.slots(0, None), self.slots(1, None), self.left)

    def forward(self):
        self.from_left.wait_recv()
        self.far_0 = self.links.send(self.slots(3, 0), self.slots(2, 0), self.right)
        self.from_right.wait_recv()
        self.far_1 = self.links.send(self.slots(1, 1), self.slots(2, 1), self.left)

    def finish(self):
        self.far_0.wait_recv()
        self.far_1.wait_recv()


class RingSum:
    def __init__(self, links, get, stage, far, near, right, left):
        self.links, self.get, self.stage, self.far, self.near = links, get, stage, far, near
        self.right, self.left, self.rows = right, left, far.shape[1]

    def put(self, at, part, value, target, device):
        rows = pl.ds(0, self.rows)
        self.stage[at, part, rows] = value.astype(self.stage.dtype)
        return self.links.send(self.stage.at[at, part, rows], target, device)

    def start(self):
        self.far_0 = self.put(1, 0, self.get(2, 0), self.far.at[0], self.left)
        self.far_1 = self.put(1, 1, self.get(2, 1), self.far.at[1], self.right)
        self.right_1 = self.put(2, 1, self.get(3, 1), self.near.at[0, 1], self.left)
        self.left_0 = self.put(0, 0, self.get(1, 0), self.near.at[1, 0], self.right)

    def forward(self):
        self.far_0.wait_recv()
        value = self.get(3, 0) + self.far[0].astype(F32)
        self.right_0 = self.put(2, 0, value, self.near.at[0, 0], self.left)
        self.far_1.wait_recv()
        value = self.get(1, 1) + self.far[1].astype(F32)
        self.left_1 = self.put(0, 1, value, self.near.at[1, 1], self.right)

    def wait(self):
        for copy in (self.right_1, self.left_0, self.right_0, self.left_1):
            copy.wait_recv()

    def total(self, part):
        return self.get(0, part) + (self.near[0, part].astype(F32) + self.near[1, part].astype(F32))


def kernel(
    width, total_rows, batch,
    image_ref, text_ref, w_image_ref, w_text_ref, scale_ref, bias_ref,
    out_image, out_text, out_loss, out_scale, out_bias,
    feat_i, feat_t, sib_t, sib_i, w_i, w_t, emb_i, emb_t, acc_i, acc_t, cross,
    stage_i, stage_t, far_r, near_r, zsend, zrecv, proj, pg, pg_sib,
    stat, st_c, st_x, st_y, st_z,
    far_p, near_p, acc_p2, stage_p2, far_p2, near_p2, sum_p2, z1, z2, z2s,
    ag1, ag2, send_sems, recv_sems, local_sems,
):
    E = width
    d = lax.axis_index("dp")
    f = lax.axis_index("fsdp")
    x, zl, y = d // 8, (d // 4) % 2, d % 4
    zh, c = f // 2, f % 2
    z = zh * 2 + zl

    def dev(x_, y_, zl_, zh_, c_):
        return (x_ * 8 + zl_ * 4 + y_, zh_ * 2 + c_)

    x_ring = [dev((x + k) % 4, y, zl, zh, c) for k in range(4)]
    y_ring = [dev(x, (y + k) % 4, zl, zh, c) for k in range(4)]
    z_side = dev(x, y, 1 - zl, zh, c)
    z_part = dev(x, y, 1 - zl, 1 - zh, c)
    z_diag = dev(x, y, zl, 1 - zh, c)
    other = dev(x, y, zl, zh, 1 - c)
    partners = x_ring[1:] + y_ring[1:] + [z_side, z_part, z_diag, other]

    slice_rows = 288
    fw = pl.multiple_of(f * slice_rows, 32)
    loads = [
        pltpu.make_async_copy(image_ref.at[pl.ds(pl.multiple_of(f * 128, 128), 128)], feat_i.at[0], local_sems.at[0]),
        pltpu.make_async_copy(text_ref, feat_t.at[0], local_sems.at[1]),
        pltpu.make_async_copy(w_image_ref, w_i.at[pl.ds(fw, slice_rows)], local_sems.at[2]),
        pltpu.make_async_copy(w_text_ref, w_t.at[pl.ds(fw, slice_rows)], local_sems.at[3]),
        pltpu.make_async_copy(
            image_ref.at[pl.ds(pl.multiple_of((zh * 2 + 1 - c) * 128, 128), 128)], sib_i, local_sems.at[4]
        ),
    ]
    for copy in loads:
        copy.start()
    barrier = pltpu.get_barrier_semaphore()
    for device in partners:
        pl.semaphore_signal(barrier, inc=1, device_id=device, device_id_type=MESH)
    pl.semaphore_wait(barrier, len(partners))
    for copy in loads:
        copy.wait()

    links = Links(send_sems, recv_sems)
    send = links.send

    def part_slots(ref, base):
        def slots(k, part):
            if part is None:
                return ref.at[base + k]
            return ref.at[base + k, pl.ds(part * 64, 64)]
        return slots

    g_i = [RingGather(links, part_slots(feat_i, 4 * p), 64, y_ring[1], y_ring[3]) for p in range(2)]
    g_t = [RingGather(links, part_slots(feat_t, 4 * p), 64, x_ring[1], x_ring[3]) for p in range(2)]

    half = slice_rows // 2
    fp = (1 - zh) * 2 + c

    def w_rows(ref, owner, which):
        return ref.at[pl.ds(pl.multiple_of(owner * slice_rows + which * half, 16), half)]

    zx_i = send(feat_i.at[0], feat_i.at[4], z_side)
    zx_t = send(feat_t.at[0], feat_t.at[4], z_part)
    w_direct = [send(w_rows(w, f, 1 - zl), w_rows(w, f, 1 - zl), z_part) for w in (w_i, w_t)]
    g_i[0].start()
    g_t[0].start()
    w_pair = [send(w.at[pl.ds(fw, slice_rows)], w.at[pl.ds(fw, slice_rows)], other) for w in (w_i, w_t)]
    sib_copy = send(feat_t.at[0], sib_t, other)

    def zero(i, carry):
        acc_t[pl.ds(pl.multiple_of(i * 128, 128), 128)] = jnp.zeros((128, E), F32)
        return carry

    lax.fori_loop(0, 16, zero, 0)
    temper = jnp.exp(jnp.full((8, 128), scale_ref[0], F32))
    t1 = temper[0:1, 0:1]
    offset = bias_ref[0]

    zx_i.wait_recv()
    g_i[1].start()
    zx_t.wait_recv()
    g_t[1].start()
    w_side, w_core = [], []
    for n, w in enumerate((w_i, w_t)):
        w_direct[n].wait_recv()
        w_side.append(send(w_rows(w, fp, zl), w_rows(w, fp, zl), z_side))
        w_core.append(send(w_rows(w, fp, zl), w_rows(w, fp, zl), other))
        (g_i, g_t)[n][0].forward()
    w_last = []
    for n, w in enumerate((w_i, w_t)):
        w_side[n].wait_recv()
        w_last.append(send(w_rows(w, fp, 1 - zl), w_rows(w, fp, 1 - zl), other))
        (g_i, g_t)[n][1].forward()

    def project(feat, w, emb, which):
        def step(g, carry):
            rows = feat[pl.ds(g * 2, 2)].reshape(256, feat.shape[2])
            p = jnp.dot(rows, w[...], preferred_element_type=F32)
            inv = lax.rsqrt(jnp.sum(p * p, axis=-1, keepdims=True) + 1e-06)
            emb[pl.ds(pl.multiple_of(g * 256, 256), 256)] = (p * inv).astype(BF)
            return carry

        lax.fori_loop(0, 4, step, 0)
        proj[which] = jnp.dot(feat[0], w[...], preferred_element_type=F32)

    for g in g_i:
        g.finish()
    w_pair[0].wait_recv()
    w_core[0].wait_recv()
    w_last[0].wait_recv()
    project(feat_i, w_i, emb_i, 0)
    for g in g_t:
        g.finish()
    w_pair[1].wait_recv()
    w_core[1].wait_recv()
    w_last[1].wait_recv()
    project(feat_t, w_t, emb_t, 1)
    emb_copy = send(emb_t.at[pl.ds(0, 1024)], emb_t.at[pl.ds(1024, 1024)], other)
    sib_copy.wait_recv()
    emb_copy.wait_recv()
    links.flush()

    k1 = t1 * LOG2E
    k0 = offset * LOG2E
    TC = 512

    def fold(v):
        return jnp.sum(v.reshape(v.shape[0] // 8, 8, v.shape[1]), axis=0)

    def tile(ic, carry):
        s_loss, s_cos, s_sig = carry
        a = emb_i[pl.ds(pl.multiple_of(ic * 256, 256), 256)]
        grad = None
        for tc in range(2048 // TC):
            rows = pl.ds(tc * TC, TC)
            b = emb_t[rows]
            cosines = lax.dot_general(a, b, LAST, preferred_element_type=F32)
            e = jnp.exp2(cosines * k1 + k0)
            s = 1.0 + e
            sig = e * pl.reciprocal(s, approx=False)
            low = sig.astype(BF)
            s_sig = s_sig + fold(sig)
            s_cos = s_cos + fold(sig * cosines)
            prod = (s[0:64] * s[64:128]) * (s[128:192] * s[192:256])
            s_loss = s_loss + fold(jnp.log(prod))
            term = jnp.dot(low, b, preferred_element_type=F32)
            grad = term if grad is None else grad + term
            acc_t[rows] += lax.dot_general(low, a, FIRST, preferred_element_type=F32)
        acc_i[pl.ds(pl.multiple_of(ic * 256, 256), 256)] = grad
        return s_loss, s_cos, s_sig

    zeros = jnp.zeros((8, TC), F32)
    s_loss, s_cos, s_sig = lax.fori_loop(0, 4, tile, (zeros, zeros, zeros))

    own_i = emb_i[0:128].astype(F32)
    own_t = emb_t[0:128].astype(F32)
    cos_d = jnp.sum(own_i * own_t, axis=-1, keepdims=True)
    l_d = cos_d * t1 + offset
    e_d = jnp.exp2(cos_d * k1 + k0)
    r_d = 1.0 / (1.0 + e_d)
    fix = -(r_d.astype(BF).astype(F32) + (e_d * r_d).astype(BF).astype(F32))

    def lanes(v):
        v = jnp.sum(v, axis=0, keepdims=True)
        return v[:, 0:128] + v[:, 128:256] + v[:, 256:384] + v[:, 384:512]

    first_lane = lax.broadcasted_iota(jnp.int32, (1, 128), 1) == 0

    def less(v, total):
        return v - jnp.where(first_lane, total, 0.0)

    stat[...] = jnp.concatenate(
        [
            less(lanes(s_loss), jnp.sum(l_d)),
            less(lanes(s_cos), jnp.sum(cos_d)),
            less(lanes(s_sig), 128.0),
            jnp.zeros((5, 128), F32),
        ],
        axis=0,
    )

    x_copy = send(acc_t.at[pl.ds(1024, 1024)], cross, other)
    st_c[c] = stat[...]
    st_copies = [send(stat, st_c.at[c], other)]

    def get_i(p):
        return lambda k, part: acc_i[pl.ds((4 * p + k) * 128 + part * 64, 64)]

    def get_t(p):
        def get(k, part):
            first = (4 * p + k) * 128 + part * 64
            return acc_t[pl.ds(first, 64)] + cross[pl.ds(first, 64)]
        return get

    r_i = [
        RingSum(links, get_i(p), stage_i.at[p], far_r.at[p], near_r.at[p], y_ring[1], y_ring[3]) for p in range(2)
    ]
    r_t = [
        RingSum(links, get_t(p), stage_t.at[p], far_r.at[2 + p], near_r.at[2 + p], x_ring[1], x_ring[3])
        for p in range(2)
    ]
    for r in (r_i[1], r_i[0]):
        r.start()
    x_copy.wait_recv()
    for r in (r_t[1], r_t[0]):
        r.start()
    for r in (r_i[1], r_t[1], r_i[0], r_t[0]):
        r.forward()
    z_copies = []
    for n, r, device in ((0, r_i[1], z_side), (1, r_t[1], z_part)):
        r.wait()
        for part in range(2):
            zsend[n, pl.ds(part * 64, 64)] = r.total(part).astype(BF)
        z_copies.append(send(zsend.at[n], zrecv.at[n], device))

    def stat_sum(ref, count):
        v = ref[0]
        for k in range(1, count):
            v = v + ref[k]
        return v

    st_copies[0].wait_recv()
    stat_c = stat_sum(st_c, 2)
    st_x[x] = stat_c
    st_cx = [send(st_x.at[x], st_x.at[x], device) for device in x_ring[1:]]

    pg_copies = []
    gain = t1 * (1.0 / total_rows)
    for n, r in ((0, r_i[0]), (1, r_t[0])):
        r.wait()
        z_copies[n].wait_recv()
        partner_emb = own_t if n == 0 else own_i
        for part in range(2):
            rows = pl.ds(part * 64, 64)
            cut = slice(part * 64, part * 64 + 64)
            g = r.total(part) + zrecv[n, rows].astype(F32) + fix[cut] * partner_emb[cut]
            g = g * gain
            p = proj[n, rows]
            inv = lax.rsqrt(jnp.sum(p * p, axis=-1, keepdims=True) + 1e-06)
            unit = p * inv
            inner = jnp.sum(unit * g, axis=-1, keepdims=True)
            pg[n, rows] = inv * (g - unit * inner)
        pg_copies.append(send(pg.at[n], pg_sib.at[n], other))

    rings = ((y_ring, y, x_ring, x), (x_ring, x, y_ring, y))
    accs = (acc_t, acc_t)
    bases = (0, 1160)
    sums = []
    links_flush_before = True
    for n in range(2):
        pg_copies[n].wait_recv()
        if links_flush_before:
            links.flush()
            links_flush_before = False
        own_f = feat_i[0] if n == 0 else feat_t[0]
        sib_f = sib_i[...] if n == 0 else sib_t[...]
        both = jnp.concatenate([own_f, sib_f], axis=0)
        hi = [pg[n].astype(BF), pg_sib[n].astype(BF)]
        lo = [(pg[n] - hi[0].astype(F32)).astype(BF), (pg_sib[n] - hi[1].astype(F32)).astype(BF)]
        for k in range(2):
            emb_i[k * 128 : k * 128 + 128] = hi[k]
            emb_i[256 + k * 128 : 384 + k * 128] = lo[k]
        base = bases[n]
        for q in range(3):
            lhs = both[:, q * 384 : (q + 1) * 384]
            acc_t[pl.ds(base + q * 384, 384)] = lax.dot_general(
                lhs, emb_i[0:256], FIRST, preferred_element_type=F32
            ) + lax.dot_general(lhs, emb_i[256:512], FIRST, preferred_element_type=F32)
        ring, r1, _, _ = rings[n]

        def get_m(k, part, base=base, r1=r1):
            first = base + (part * 2 + c) * slice_rows + ((r1 + k) % 4) * 72
            return acc_t[pl.ds(pl.multiple_of(first, 8), 80)]

        s = RingSum(links, get_m, stage_i.at[n], far_p.at[n], near_p.at[n], ring[1], ring[3])
        s.start()
        sums.append(s)
    for copy in st_cx:
        copy.wait_recv()
    stat_x = stat_sum(st_x, 4)
    st_y[y] = stat_x
    st_cy = [send(st_y.at[y], st_y.at[y], device) for device in y_ring[1:]]
    for s in sums:
        s.forward()
    sums2 = []
    for n in range(2):
        sums[n].wait()
        for part in range(2):
            acc_p2[n, part, 0:72] = sums[n].total(part)[0:72]
            acc_p2[n, part, 72:96] = jnp.zeros((24, E), F32)
        _, _, ring, r2 = rings[n]

        def get_2(k, part, n=n, r2=r2):
            return acc_p2[n, part, pl.ds(pl.multiple_of(((r2 + k) % 4) * 24, 8), 24)]

        s = RingSum(links, get_2, stage_p2.at[n], far_p2.at[n], near_p2.at[n], ring[1], ring[3])
        s.start()
        sums2.append(s)
    for copy in st_cy:
        copy.wait_recv()
    stat_y = stat_sum(st_y, 4)
    st_z[z] = stat_y
    st_cz = [send(st_z.at[z], st_z.at[z], device) for device in (z_side, z_part, z_diag)]
    for s in sums2:
        s.forward()
    z1_copies = []
    for n in range(2):
        sums2[n].wait()
        for part in range(2):
            sum_p2[n, part] = sums2[n].total(part)
        z1_copies.append(send(sum_p2.at[n, 1 - zh], z1.at[n], z_part))
    z2_copies = []
    for n in range(2):
        z1_copies[n].wait_recv()
        z2s[n] = sum_p2[n, zh] + z1[n]
        z2_copies.append(send(z2s.at[n], z2.at[n], z_side))
    gathers = []
    for n in range(2):
        z2_copies[n].wait_recv()
        ag1[n, 0] = z2s[n] + z2[n]
        ring = rings[n][2]

        def slots1(k, part, n=n):
            if part is None:
                return ag1.at[n, k]
            return ag1.at[n, k, pl.ds(part * 16, 16 - part * 8)]

        g = RingGather(links, slots1, 16, ring[1], ring[3])
        g.start()
        gathers.append(g)
    for g in gathers:
        g.forward()
    gathers2 = []
    for n in range(2):
        gathers[n].finish()
        ring, _, _, r2 = rings[n]
        for k in range(4):
            ag2[n, 0, pl.ds(pl.multiple_of(((r2 + k) % 4) * 24, 8), 24)] = ag1[n, k]

        def slots2(k, part, n=n):
            if part is None:
                return ag2.at[n, k, pl.ds(0, 72)]
            return ag2.at[n, k, pl.ds(part * 40, 40 - part * 8)]

        g = RingGather(links, slots2, 40, ring[1], ring[3])
        g.start()
        gathers2.append(g)

    def put(n, k):
        out = (out_image, out_text)[n]
        r1 = rings[n][1]
        copy = pltpu.make_async_copy(
            ag2.at[n, k, pl.ds(0, 72)],
            out.at[pl.ds(pl.multiple_of(((r1 + k) % 4) * 72, 8), 72)],
            local_sems.at[5 + n * 4 + k],
        )
        copy.start()
        return copy

    puts = [put(n, 0) for n in range(2)]
    for copy in st_cz:
        copy.wait_recv()
    stat_z = stat_sum(st_z, 4)
    out_loss[0] = jnp.sum(stat_z[0:1]) * (1.0 / total_rows / total_rows)
    out_scale[0] = jnp.sum(stat_z[1:2] * temper[0:1]) * (1.0 / total_rows)
    out_bias[0] = jnp.sum(stat_z[2:3]) * (1.0 / total_rows)
    for g in gathers2:
        g.forward()
    puts += [put(n, k) for n in range(2) for k in (1, 3)]
    for n in range(2):
        gathers2[n].finish()
        puts.append(put(n, 2))
    for copy in puts:
        copy.wait()
    links.flush()


def solution(mesh):
    def body(image_feats, text_feats, w_image, w_text, logit_scale, logit_bias):
        width = w_image.shape[1]
        total = image_feats.shape[0] * mesh.shape["dp"]
        E = width
        hbm = pl.BlockSpec(memory_space=pl.ANY)
        smem = pl.BlockSpec(memory_space=pltpu.SMEM)
        V = pltpu.VMEM
        one = jax.ShapeDtypeStruct((1,), F32)
        outs = pl.pallas_call(
            functools.partial(kernel, width, total, 512),
            out_shape=(
                jax.ShapeDtypeStruct(w_image.shape, F32),
                jax.ShapeDtypeStruct(w_text.shape, F32),
                one, one, one,
            ),
            in_specs=[hbm] * 4 + [smem] * 2,
            out_specs=(hbm, hbm, smem, smem, smem),
            scratch_shapes=[
                V((8, 128, E), BF),
                V((8, 128, E), BF),
                V((128, E), BF),
                V((128, E), BF),
                V((1152, E), BF),
                V((1152, E), BF),
                V((1024, E), BF),
                V((2048, E), BF),
                V((1024, E), F32),
                V((2328, E), F32),
                V((1024, E), F32),
                V((2, 3, 2, 80, E), BF),
                V((2, 3, 2, 64, E), BF),
                V((4, 2, 64, E), BF),
                V((4, 2, 2, 64, E), BF),
                V((2, 128, E), BF),
                V((2, 128, E), BF),
                V((2, 128, E), F32),
                V((2, 128, E), F32),
                V((2, 128, E), F32),
                V((8, 128), F32),
                V((2, 8, 128), F32),
                V((4, 8, 128), F32),
                V((4, 8, 128), F32),
                V((4, 8, 128), F32),
                V((2, 2, 80, E), BF),
                V((2, 2, 2, 80, E), BF),
                V((2, 2, 96, E), F32),
                V((2, 3, 2, 24, E), F32),
                V((2, 2, 24, E), F32),
                V((2, 2, 2, 24, E), F32),
                V((2, 2, 24, E), F32),
                V((2, 24, E), F32),
                V((2, 24, E), F32),
                V((2, 24, E), F32),
                V((2, 4, 24, E), F32),
                V((2, 4, 96, E), F32),
                pltpu.SemaphoreType.DMA((120,)),
                pltpu.SemaphoreType.DMA((120,)),
                pltpu.SemaphoreType.DMA((16,)),
            ],
            compiler_params=pltpu.CompilerParams(
                collective_id=0, has_side_effects=True, vmem_limit_bytes=63 * 1024 * 1024
            ),
            cost_estimate=pl.CostEstimate(flops=16_000_000_000, bytes_accessed=20_000_000, transcendentals=6_000_000),
        )(image_feats, text_feats, w_image, w_text, logit_scale, logit_bias)
        g_image, g_text, loss, g_scale, g_bias = outs
        return (loss, g_image, g_text, g_scale, g_bias)

    placed = (P("dp", None), P(("dp", "fsdp"), None), P("fsdp", None), P("fsdp", None), P(), P())
    return jax.shard_map(
        body,
        mesh=mesh,
        in_specs=placed,
        out_specs=(P(), P("fsdp", None), P("fsdp", None), P(), P()),
        check_vma=False,
    )
```

```python
import functools

import jax
import jax.numpy as jnp
from jax import lax
from jax.experimental import pallas as pl
from jax.experimental.pallas import tpu as pltpu
from jax.sharding import PartitionSpec as P

MESH = pl.DeviceIdType.MESH
BF = jnp.bfloat16
F32 = jnp.float32
LAST = (((1,), (1,)), ((), ()))
FIRST = (((0,), (0,)), ((), ()))
LOG2E = 1.4426950408889634


class Links:
    def __init__(self, send_sems, recv_sems):
        self.send_sems, self.recv_sems, self.used, self.open = send_sems, recv_sems, 0, []

    def send(self, src, dst, device):
        copy = pltpu.make_async_remote_copy(
            src_ref=src,
            dst_ref=dst,
            send_sem=self.send_sems.at[self.used],
            recv_sem=self.recv_sems.at[self.used],
            device_id=device,
            device_id_type=MESH,
        )
        self.used += 1
        copy.start()
        self.open.append(copy)
        return copy

    def flush(self):
        for copy in self.open:
            copy.wait_send()
        self.open = []


class RingGather:
    def __init__(self, links, slots, right, left):
        self.links, self.slots, self.right, self.left = links, slots, right, left

    def start(self):
        self.from_left = self.links.send(self.slots(0, None), self.slots(3, None), self.right)
        self.from_right = self.links.send(self.slots(0, None), self.slots(1, None), self.left)

    def forward(self):
        self.from_left.wait_recv()
        self.far_0 = self.links.send(self.slots(3, 0), self.slots(2, 0), self.right)
        self.from_right.wait_recv()
        self.far_1 = self.links.send(self.slots(1, 1), self.slots(2, 1), self.left)

    def finish(self):
        self.far_0.wait_recv()
        self.far_1.wait_recv()


class RingSum:
    def __init__(self, links, get, stage, far, near, cuts, right, left):
        self.links, self.get, self.stage, self.far, self.near = links, get, stage, far, near
        self.right, self.left, self.cuts = right, left, cuts

    def put(self, at, part, value, target, device):
        rows = pl.ds(0, self.cuts[part])
        self.stage[at, part, rows] = value.astype(self.stage.dtype)
        return self.links.send(self.stage.at[at, part, rows], target.at[rows], device)

    def came(self, ref, part):
        return ref[0 : self.cuts[part]].astype(F32)

    def start_far(self):
        self.far_0 = self.put(1, 0, self.get(2, 0), self.far.at[0], self.left)
        self.far_1 = self.put(1, 1, self.get(2, 1), self.far.at[1], self.right)

    def start_left(self):
        self.right_1 = self.put(2, 1, self.get(3, 1), self.near.at[0, 1], self.left)

    def start_right(self):
        self.left_0 = self.put(0, 0, self.get(1, 0), self.near.at[1, 0], self.right)

    def sum_left(self):
        self.far_0.wait_recv()
        value = self.get(3, 0) + self.came(self.far.at[0], 0)
        self.right_0 = self.put(2, 0, value, self.near.at[0, 0], self.left)

    def sum_right(self):
        self.far_1.wait_recv()
        value = self.get(1, 1) + self.came(self.far.at[1], 1)
        self.left_1 = self.put(0, 1, value, self.near.at[1, 1], self.right)

    def start(self):
        self.start_far()
        self.start_left()
        self.start_right()

    def forward(self):
        self.sum_left()
        self.sum_right()

    def wait(self):
        for copy in (self.right_1, self.left_0, self.right_0, self.left_1):
            copy.wait_recv()

    def total(self, part):
        return self.get(0, part) + (self.came(self.near.at[0, part], part) + self.came(self.near.at[1, part], part))


def kernel(
    width, total_rows,
    image_ref, text_ref, w_image_ref, w_text_ref, scale_ref, bias_ref,
    out_image, out_text, out_loss, out_scale, out_bias,
    feat_i, feat_t, peer_i, peer_t, w_i, w_t, emb_i, emb_t, acc_i, acc_t, cross,
    stage_i, stage_t, far_r, near_r, zsend, zrecv, proj, pg,
    stat, st_c, st_x, st_y, st_z,
    far_p, near_p, acc_p2, stage_p2, far_p2, near_p2, z2, z2s,
    ag1, ag2, send_sems, recv_sems, local_sems,
):
    E = width
    d = lax.axis_index("dp")
    f = lax.axis_index("fsdp")
    x, zl, y = d // 8, (d // 4) % 2, d % 4
    zh, c = f // 2, f % 2
    z = zh * 2 + zl

    def dev(x_, y_, zl_, zh_, c_):
        return (x_ * 8 + zl_ * 4 + y_, zh_ * 2 + c_)

    x_ring = [dev((x + k) % 4, y, zl, zh, c) for k in range(4)]
    y_ring = [dev(x, (y + k) % 4, zl, zh, c) for k in range(4)]
    z_side = dev(x, y, 1 - zl, zh, c)
    z_part = dev(x, y, 1 - zl, 1 - zh, c)
    z_diag = dev(x, y, zl, 1 - zh, c)
    other = dev(x, y, zl, zh, 1 - c)
    partners = x_ring[1:] + y_ring[1:] + [z_side, z_part, z_diag, other]

    slice_rows = 288
    fw = pl.multiple_of(f * slice_rows, 32)
    loads = [
        pltpu.make_async_copy(image_ref.at[pl.ds(pl.multiple_of(f * 128, 128), 128)], feat_i.at[0], local_sems.at[0]),
        pltpu.make_async_copy(text_ref, feat_t.at[0], local_sems.at[1]),
        pltpu.make_async_copy(w_image_ref, w_i.at[pl.ds(fw, slice_rows)], local_sems.at[2]),
        pltpu.make_async_copy(w_text_ref, w_t.at[pl.ds(fw, slice_rows)], local_sems.at[3]),
        pltpu.make_async_copy(
            image_ref.at[pl.ds(pl.multiple_of((zh * 2 + 1 - c) * 128, 128), 128)], peer_i.at[0], local_sems.at[4]
        ),
    ]
    for copy in loads:
        copy.start()
    barrier = pltpu.get_barrier_semaphore()
    for device in partners:
        pl.semaphore_signal(barrier, inc=1, device_id=device, device_id_type=MESH)
    pl.semaphore_wait(barrier, len(partners))
    for copy in loads:
        copy.wait()

    links = Links(send_sems, recv_sems)
    send = links.send

    def part_slots(ref, p):
        def slots(k, part):
            if part is None:
                return ref.at[2 * k + p]
            return ref.at[2 * k + p, pl.ds(part * 64, 64)]
        return slots

    g_i = [RingGather(links, part_slots(feat_i, p), y_ring[1], y_ring[3]) for p in range(2)]
    g_t = [RingGather(links, part_slots(feat_t, p), x_ring[1], x_ring[3]) for p in range(2)]

    half = slice_rows // 2
    fp = (1 - zh) * 2 + c

    def w_rows(ref, owner, which):
        return ref.at[pl.ds(pl.multiple_of(owner * slice_rows + which * half, 16), half)]

    def w_send(w, owner, which, device):
        return send(w_rows(w, owner, which), w_rows(w, owner, which), device)

    zx_t = send(feat_t.at[0], feat_t.at[1], z_part)
    zx_i = send(feat_i.at[0], feat_i.at[1], z_side)
    wt_direct = w_send(w_t, f, 1 - zl, z_part)
    wi_direct = w_send(w_i, f, 1 - zl, z_part)
    g_t[0].start()
    g_i[0].start()
    w_pair = [send(w.at[pl.ds(fw, slice_rows)], w.at[pl.ds(fw, slice_rows)], other) for w in (w_t, w_i)]
    peers = [send(feat_t.at[0], peer_t.at[0], other)]

    def zero(i, carry):
        acc_t[pl.ds(pl.multiple_of(i * 128, 128), 128)] = jnp.zeros((128, E), F32)
        acc_i[pl.ds(pl.multiple_of(i * 64, 64), 64)] = jnp.zeros((64, E), F32)
        return carry

    lax.fori_loop(0, 16, zero, 0)
    temper = jnp.exp(jnp.full((8, 128), scale_ref[0], F32))
    t1 = temper[0:1, 0:1]
    offset = bias_ref[0]

    zx_t.wait_recv()
    g_t[1].start()
    zx_i.wait_recv()
    g_i[1].start()
    wt_direct.wait_recv()
    wt_side = w_send(w_t, fp, zl, z_side)
    wt_core = w_send(w_t, fp, zl, other)
    g_t[0].forward()
    g_i[0].forward()
    wi_direct.wait_recv()
    wi_side = w_send(w_i, fp, zl, z_side)
    wi_core = w_send(w_i, fp, zl, other)
    wt_side.wait_recv()
    wt_last = w_send(w_t, fp, 1 - zl, other)
    g_t[1].forward()
    g_i[1].forward()
    wi_side.wait_recv()
    wi_last = w_send(w_i, fp, 1 - zl, other)
    peers.append(send(feat_t.at[1], peer_t.at[1], other))
    zpeer = send(feat_i.at[0], peer_i.at[1], z_part)

    def project(feat, w, k):
        p = jnp.dot(feat[2 * k : 2 * k + 2].reshape(256, feat.shape[2]), w[...], preferred_element_type=F32)
        inv = lax.rsqrt(jnp.sum(p * p, axis=-1, keepdims=True) + 1e-06)
        return p, (p * inv).astype(BF)

    for copy in (w_pair[0], wt_core, wt_last):
        copy.wait_recv()
    emb_copies = []
    for k in (0, 3, 1, 2):
        if k == 2:
            g_t[0].finish()
            g_t[1].finish()
        p, emb = project(feat_t, w_t, k)
        if k == 0:
            proj[1] = p[0:128]
        emb_t[k * 512 : k * 512 + 256] = emb
        emb_copies.append(
            send(emb_t.at[pl.ds(k * 512, 256)], emb_t.at[pl.ds(k * 512 + 256, 256)], other)
        )
    for copy in (w_pair[1], wi_core, wi_last):
        copy.wait_recv()
    for k in (0, 3, 1, 2):
        if k == 2:
            g_i[0].finish()
            g_i[1].finish()
        p, emb = project(feat_i, w_i, k)
        if k == 0:
            proj[0] = p[0:128]
        emb_i[k * 256 : k * 256 + 256] = emb
    for copy in emb_copies:
        copy.wait_recv()
    zpeer.wait_recv()
    peers.append(send(peer_i.at[1], peer_i.at[2], other))
    for copy in peers[0:2]:
        copy.wait_recv()

    k1 = t1 * LOG2E
    k0 = offset * LOG2E

    def fold(v):
        return jnp.sum(v.reshape(v.shape[0] // 8, 8, v.shape[1]), axis=0)

    def tile(ki, kt, carry):
        s_loss, s_cos, s_sig = carry
        rows_i = pl.ds(ki * 256, 256) if isinstance(ki, int) else pl.ds(pl.multiple_of(ki * 256, 256), 256)
        rows_t = pl.ds(kt * 512, 512) if isinstance(kt, int) else pl.ds(pl.multiple_of(kt * 512, 512), 512)
        a, b = emb_i[rows_i], emb_t[rows_t]
        cosines = lax.dot_general(a, b, LAST, preferred_element_type=F32)
        e = jnp.exp2(cosines * k1 + k0)
        s = 1.0 + e
        sig = e * pl.reciprocal(s, approx=False)
        low = sig.astype(BF)
        s_sig = s_sig + fold(sig)
        s_cos = s_cos + fold(sig * cosines)
        prod = (s[0:64] * s[64:128]) * (s[128:192] * s[192:256])
        s_loss = s_loss + fold(jnp.log(prod))
        acc_i[rows_i] += jnp.dot(low, b, preferred_element_type=F32)
        acc_t[rows_t] += lax.dot_general(low, a, FIRST, preferred_element_type=F32)
        return s_loss, s_cos, s_sig

    def get_i(p):
        return lambda k, part: acc_i[pl.ds(k * 256 + p * 128 + part * 64, 64)]

    def get_t(p):
        def get(k, part):
            at = p * 128 + part * 64
            return acc_t[pl.ds(k * 512 + at, 64)] + cross[pl.ds(k * 256 + at, 64)]
        return get

    cuts = (64, 64)
    r_i = [
        RingSum(links, get_i(p), stage_i.at[p], far_r.at[p], near_r.at[p], cuts, y_ring[1], y_ring[3])
        for p in range(2)
    ]
    r_t = [
        RingSum(links, get_t(p), stage_t.at[p], far_r.at[2 + p], near_r.at[2 + p], cuts, x_ring[1], x_ring[3])
        for p in range(2)
    ]

    def cross_send(k):
        return send(acc_t.at[pl.ds(k * 512 + 256, 256)], cross.at[pl.ds(k * 256, 256)], other)

    zeros = jnp.zeros((8, 512), F32)
    sums = (zeros, zeros, zeros)
    sums = lax.fori_loop(0, 4, lambda i, s: tile(i, 2, s), sums)
    cross_2 = cross_send(2)
    sums = lax.fori_loop(0, 3, lambda i, s: tile(2, (i + 3) % 4, s), sums)
    for r in (r_i[1], r_i[0]):
        r.start_far()
    cross_2.wait_recv()
    for r in (r_t[1], r_t[0]):
        r.start_far()
    sums = lax.fori_loop(0, 3, lambda i, s: tile((i + 3) % 4, 3, s), sums)
    cross_3 = cross_send(3)
    sums = lax.fori_loop(0, 2, lambda i, s: tile(3, i, s), sums)
    for r in (r_i[1], r_i[0]):
        r.start_left()
    cross_3.wait_recv()
    for r in (r_t[1], r_t[0]):
        r.start_left()
    for r in (r_i[1], r_t[1], r_i[0], r_t[0]):
        r.sum_left()
    sums = lax.fori_loop(0, 2, lambda i, s: tile(i, 1, s), sums)
    cross_1 = cross_send(1)
    sums = tile(1, 0, sums)
    for r in (r_i[1], r_i[0]):
        r.start_right()
    cross_1.wait_recv()
    for r in (r_t[1], r_t[0]):
        r.start_right()
    for r in (r_i[1], r_t[1], r_i[0], r_t[0]):
        r.sum_right()
    s_loss, s_cos, s_sig = tile(0, 0, sums)
    cross_0 = cross_send(0)

    own_i = emb_i[0:128].astype(F32)
    own_t = emb_t[0:128].astype(F32)
    cos_d = jnp.sum(own_i * own_t, axis=-1, keepdims=True)
    l_d = cos_d * t1 + offset
    e_d = jnp.exp2(cos_d * k1 + k0)
    r_d = 1.0 / (1.0 + e_d)
    fix = -(r_d.astype(BF).astype(F32) + (e_d * r_d).astype(BF).astype(F32))

    def lanes(v):
        v = jnp.sum(v, axis=0, keepdims=True)
        return v[:, 0:128] + v[:, 128:256] + v[:, 256:384] + v[:, 384:512]

    first_lane = lax.broadcasted_iota(jnp.int32, (1, 128), 1) == 0

    def less(v, total):
        return v - jnp.where(first_lane, total, 0.0)

    stat[...] = jnp.concatenate(
        [
            less(lanes(s_loss), jnp.sum(l_d)),
            less(lanes(s_cos), jnp.sum(cos_d)),
            less(lanes(s_sig), 128.0),
            jnp.zeros((5, 128), F32),
        ],
        axis=0,
    )

    st_c[c] = stat[...]
    st_copies = [send(stat, st_c.at[c], other)]
    cross_0.wait_recv()
    z_copies = []
    for n, r, device in ((0, r_i[1], z_side), (1, r_t[1], z_part)):
        r.wait()
        for part in range(2):
            zsend[n, pl.ds(part * 64, 64)] = r.total(part).astype(BF)
        z_copies.append(send(zsend.at[n], zrecv.at[n], device))

    def stat_sum(ref, count):
        v = ref[0]
        for k in range(1, count):
            v = v + ref[k]
        return v

    st_copies[0].wait_recv()
    stat_c = stat_sum(st_c, 2)
    st_x[x] = stat_c
    st_cx = [send(st_x.at[x], st_x.at[x], device) for device in x_ring[1:]]

    core_copies, part_copies = [], []
    gain = t1 * (1.0 / total_rows)
    for n, r in ((0, r_i[0]), (1, r_t[0])):
        r.wait()
        z_copies[n].wait_recv()
        partner_emb = own_t if n == 0 else own_i
        for part in range(2):
            rows = pl.ds(part * 64, 64)
            cut = slice(part * 64, part * 64 + 64)
            g = r.total(part) + zrecv[n, rows].astype(F32) + fix[cut] * partner_emb[cut]
            g = g * gain
            p = proj[n, rows]
            inv = lax.rsqrt(jnp.sum(p * p, axis=-1, keepdims=True) + 1e-06)
            unit = p * inv
            inner = jnp.sum(unit * g, axis=-1, keepdims=True)
            pg[n, 0, rows] = (inv * (g - unit * inner)).astype(BF)
        part_copies.append(send(pg.at[n, 0], pg.at[n, 2], z_part))
        core_copies.append(send(pg.at[n, 0], pg.at[n, 1], other))

    peers[2].wait_recv()
    rings = ((y_ring, y, x_ring, x), (x_ring, x, y_ring, y))
    bases = (0, 1160)
    last_copies = []
    for n in range(2):
        part_copies[n].wait_recv()
        last_copies.append(send(pg.at[n, 2], pg.at[n, 3], other))
    links.flush()
    sums = []
    for n in range(2):
        core_copies[n].wait_recv()
        last_copies[n].wait_recv()
        if n == 0:
            lhs = jnp.concatenate([feat_i[0], peer_i[0], peer_i[1], peer_i[2]], axis=0)
        else:
            lhs = jnp.concatenate([feat_t[0], peer_t[0], feat_t[1], peer_t[1]], axis=0)
        rhs = pg[n].reshape(512, E)
        base = bases[n]
        for q in range(3):
            acc_t[pl.ds(base + q * 384, 384)] = lax.dot_general(
                lhs[:, q * 384 : (q + 1) * 384], rhs, FIRST, preferred_element_type=F32
            )
        ring, r1, _, _ = rings[n]

        def get_m(k, part, base=base, r1=r1):
            first = base + f * slice_rows + ((r1 + k) % 4) * 72 + part * 48
            return acc_t[pl.ds(pl.multiple_of(first, 8), 48 - part * 16)]

        s = RingSum(links, get_m, stage_i.at[n], far_p.at[n], near_p.at[n], (48, 32), ring[1], ring[3])
        s.start()
        sums.append(s)
    for copy in st_cx:
        copy.wait_recv()
    stat_x = stat_sum(st_x, 4)
    st_y[y] = stat_x
    st_cy = [send(st_y.at[y], st_y.at[y], device) for device in y_ring[1:]]
    for s in sums:
        s.forward()
    sums2 = []
    for n in range(2):
        sums[n].wait()
        acc_p2[n, 0:48] = sums[n].total(0)
        acc_p2[n, 48:72] = sums[n].total(1)[0:24]
        acc_p2[n, 72:96] = jnp.zeros((24, E), F32)
        _, _, ring, r2 = rings[n]

        def get_2(k, part, n=n, r2=r2):
            first = ((r2 + k) % 4) * 24 + part * 16
            return acc_p2[n, pl.ds(pl.multiple_of(first, 8), 16 - part * 8)]

        s = RingSum(links, get_2, stage_p2.at[n], far_p2.at[n], near_p2.at[n], (16, 8), ring[1], ring[3])
        s.start()
        sums2.append(s)
    for copy in st_cy:
        copy.wait_recv()
    stat_y = stat_sum(st_y, 4)
    st_z[z] = stat_y
    st_cz = [send(st_z.at[z], st_z.at[z], device) for device in (z_side, z_part, z_diag)]
    for s in sums2:
        s.forward()
    z2_copies = []
    for n in range(2):
        sums2[n].wait()
        for part in range(2):
            z2s[n, pl.ds(part * 16, 16 - part * 8)] = sums2[n].total(part)
        z2_copies.append(send(z2s.at[n], z2.at[n], z_side))
    gathers = []
    for n in range(2):
        z2_copies[n].wait_recv()
        ag1[n, 0] = z2s[n] + z2[n]
        ring = rings[n][2]

        def slots1(k, part, n=n):
            if part is None:
                return ag1.at[n, k]
            return ag1.at[n, k, pl.ds(part * 16, 16 - part * 8)]

        g = RingGather(links, slots1, ring[1], ring[3])
        g.start()
        gathers.append(g)
    for g in gathers:
        g.forward()
    gathers2 = []
    for n in range(2):
        gathers[n].finish()
        ring, _, _, r2 = rings[n]
        for k in range(4):
            ag2[n, 0, pl.ds(pl.multiple_of(((r2 + k) % 4) * 24, 8), 24)] = ag1[n, k]

        def slots2(k, part, n=n):
            if part is None:
                return ag2.at[n, k, pl.ds(0, 72)]
            return ag2.at[n, k, pl.ds(part * 40, 40 - part * 8)]

        g = RingGather(links, slots2, ring[1], ring[3])
        g.start()
        gathers2.append(g)

    def put(n, k):
        out = (out_image, out_text)[n]
        r1 = rings[n][1]
        copy = pltpu.make_async_copy(
            ag2.at[n, k, pl.ds(0, 72)],
            out.at[pl.ds(pl.multiple_of(((r1 + k) % 4) * 72, 8), 72)],
            local_sems.at[5 + n * 4 + k],
        )
        copy.start()
        return copy

    puts = [put(n, 0) for n in range(2)]
    for copy in st_cz:
        copy.wait_recv()
    stat_z = stat_sum(st_z, 4)
    out_loss[0] = jnp.sum(stat_z[0:1]) * (1.0 / total_rows / total_rows)
    out_scale[0] = jnp.sum(stat_z[1:2] * temper[0:1]) * (1.0 / total_rows)
    out_bias[0] = jnp.sum(stat_z[2:3]) * (1.0 / total_rows)
    for g in gathers2:
        g.forward()
    puts += [put(n, k) for n in range(2) for k in (1, 3)]
    for n in range(2):
        gathers2[n].finish()
        puts.append(put(n, 2))
    for copy in puts:
        copy.wait()
    links.flush()


def solution(mesh):
    def body(image_feats, text_feats, w_image, w_text, logit_scale, logit_bias):
        width = w_image.shape[1]
        total = image_feats.shape[0] * mesh.shape["dp"]
        E = width
        hbm = pl.BlockSpec(memory_space=pl.ANY)
        smem = pl.BlockSpec(memory_space=pltpu.SMEM)
        V = pltpu.VMEM
        one = jax.ShapeDtypeStruct((1,), F32)
        outs = pl.pallas_call(
            functools.partial(kernel, width, total),
            out_shape=(
                jax.ShapeDtypeStruct(w_image.shape, F32),
                jax.ShapeDtypeStruct(w_text.shape, F32),
                one, one, one,
            ),
            in_specs=[hbm] * 4 + [smem] * 2,
            out_specs=(hbm, hbm, smem, smem, smem),
            scratch_shapes=[
                V((8, 128, E), BF),
                V((8, 128, E), BF),
                V((3, 128, E), BF),
                V((2, 128, E), BF),
                V((1152, E), BF),
                V((1152, E), BF),
                V((1024, E), BF),
                V((2048, E), BF),
                V((1024, E), F32),
                V((2328, E), F32),
                V((1024, E), F32),
                V((2, 3, 2, 64, E), BF),
                V((2, 3, 2, 64, E), BF),
                V((4, 2, 64, E), BF),
                V((4, 2, 2, 64, E), BF),
                V((2, 128, E), BF),
                V((2, 128, E), BF),
                V((2, 128, E), F32),
                V((2, 4, 128, E), BF),
                V((8, 128), F32),
                V((2, 8, 128), F32),
                V((4, 8, 128), F32),
                V((4, 8, 128), F32),
                V((4, 8, 128), F32),
                V((2, 2, 48, E), BF),
                V((2, 2, 2, 48, E), BF),
                V((2, 96, E), F32),
                V((2, 3, 2, 16, E), F32),
                V((2, 2, 16, E), F32),
                V((2, 2, 2, 16, E), F32),
                V((2, 24, E), F32),
                V((2, 24, E), F32),
                V((2, 4, 24, E), F32),
                V((2, 4, 96, E), F32),
                pltpu.SemaphoreType.DMA((200,)),
                pltpu.SemaphoreType.DMA((200,)),
                pltpu.SemaphoreType.DMA((16,)),
            ],
            compiler_params=pltpu.CompilerParams(
                collective_id=0, has_side_effects=True, vmem_limit_bytes=63 * 1024 * 1024
            ),
            cost_estimate=pl.CostEstimate(flops=16_000_000_000, bytes_accessed=20_000_000, transcendentals=6_000_000),
        )(image_feats, text_feats, w_image, w_text, logit_scale, logit_bias)
        g_image, g_text, loss, g_scale, g_bias = outs
        return (loss, g_image, g_text, g_scale, g_bias)

    placed = (P("dp", None), P(("dp", "fsdp"), None), P("fsdp", None), P("fsdp", None), P(), P())
    return jax.shard_map(
        body,
        mesh=mesh,
        in_specs=placed,
        out_specs=(P(), P("fsdp", None), P("fsdp", None), P(), P()),
        check_vma=False,
    )
```

```python
import functools

import jax
import jax.numpy as jnp
from jax import lax
from jax.experimental import pallas as pl
from jax.experimental.pallas import tpu as pltpu
from jax.sharding import PartitionSpec as P

MESH = pl.DeviceIdType.MESH
BF = jnp.bfloat16
F32 = jnp.float32
LAST = (((1,), (1,)), ((), ()))
FIRST = (((0,), (0,)), ((), ()))
LOG2E = 1.4426950408889634
PLACE = {(0, 0): 0, (0, 1): 1, (3, 0): 2, (1, 0): 3, (3, 1): 4, (1, 1): 5, (2, 1): 6, (2, 0): 7}


class Links:
    def __init__(self, send_sems, recv_sems):
        self.send_sems, self.recv_sems, self.used, self.open = send_sems, recv_sems, 0, []

    def send(self, src, dst, device):
        copy = pltpu.make_async_remote_copy(
            src_ref=src,
            dst_ref=dst,
            send_sem=self.send_sems.at[self.used],
            recv_sem=self.recv_sems.at[self.used],
            device_id=device,
            device_id_type=MESH,
        )
        self.used += 1
        copy.start()
        self.open.append(copy)
        return copy

    def flush(self):
        for copy in self.open:
            copy.wait_send()
        self.open = []


class RingGather:
    def __init__(self, links, slots, right, left):
        self.links, self.slots, self.right, self.left = links, slots, right, left

    def start(self):
        self.from_left = self.links.send(self.slots(0, None), self.slots(3, None), self.right)
        self.from_right = self.links.send(self.slots(0, None), self.slots(1, None), self.left)

    def forward(self):
        self.from_left.wait_recv()
        self.far_0 = self.links.send(self.slots(3, 0), self.slots(2, 0), self.right)
        self.from_right.wait_recv()
        self.far_1 = self.links.send(self.slots(1, 1), self.slots(2, 1), self.left)

    def finish(self):
        self.far_0.wait_recv()
        self.far_1.wait_recv()


class RingSum:
    def __init__(self, links, get, stage, far, near, cuts, right, left):
        self.links, self.get, self.stage, self.far, self.near = links, get, stage, far, near
        self.right, self.left, self.cuts = right, left, cuts

    def put(self, at, part, value, target, device):
        rows = pl.ds(0, self.cuts[part])
        self.stage[at, part, rows] = value.astype(self.stage.dtype)
        return self.links.send(self.stage.at[at, part, rows], target.at[rows], device)

    def came(self, ref, part):
        return ref[0 : self.cuts[part]].astype(F32)

    def start_far(self):
        self.far_0 = self.put(1, 0, self.get(2, 0), self.far.at[0], self.left)
        self.far_1 = self.put(1, 1, self.get(2, 1), self.far.at[1], self.right)

    def start_left(self):
        self.right_1 = self.put(2, 1, self.get(3, 1), self.near.at[0, 1], self.left)

    def start_right(self):
        self.left_0 = self.put(0, 0, self.get(1, 0), self.near.at[1, 0], self.right)

    def sum_left(self):
        self.far_0.wait_recv()
        value = self.get(3, 0) + self.came(self.far.at[0], 0)
        self.right_0 = self.put(2, 0, value, self.near.at[0, 0], self.left)

    def sum_right(self):
        self.far_1.wait_recv()
        value = self.get(1, 1) + self.came(self.far.at[1], 1)
        self.left_1 = self.put(0, 1, value, self.near.at[1, 1], self.right)

    def start(self):
        self.start_far()
        self.start_left()
        self.start_right()

    def forward(self):
        self.sum_left()
        self.sum_right()

    def wait(self):
        for copy in (self.right_1, self.left_0, self.right_0, self.left_1):
            copy.wait_recv()

    def total(self, part):
        return self.get(0, part) + (self.came(self.near.at[0, part], part) + self.came(self.near.at[1, part], part))


def kernel(
    width, total_rows,
    image_ref, text_ref, w_image_ref, w_text_ref, scale_ref, bias_ref,
    out_image, out_text, out_loss, out_scale, out_bias,
    feat_i, feat_t, peer_i, peer_t, w_i, w_t, emb_i, emb_t, acc_i, acc_t, cross,
    stage_i, stage_t, far_r, near_r, zsend, zrecv, proj, pg,
    stat, st_c, st_x, st_y, st_z,
    far_p, near_p, acc_p2, stage_p2, far_p2, near_p2, z2, z2s,
    ag1, ag2, send_sems, recv_sems, local_sems,
):
    E = width
    d = lax.axis_index("dp")
    f = lax.axis_index("fsdp")
    x, zl, y = d // 8, (d // 4) % 2, d % 4
    zh, c = f // 2, f % 2
    z = zh * 2 + zl

    def dev(x_, y_, zl_, zh_, c_):
        return (x_ * 8 + zl_ * 4 + y_, zh_ * 2 + c_)

    x_ring = [dev((x + k) % 4, y, zl, zh, c) for k in range(4)]
    y_ring = [dev(x, (y + k) % 4, zl, zh, c) for k in range(4)]
    z_side = dev(x, y, 1 - zl, zh, c)
    z_part = dev(x, y, 1 - zl, 1 - zh, c)
    z_diag = dev(x, y, zl, 1 - zh, c)
    other = dev(x, y, zl, zh, 1 - c)
    partners = x_ring[1:] + y_ring[1:] + [z_side, z_part, z_diag, other]

    slice_rows = 288
    fw = pl.multiple_of(f * slice_rows, 32)
    loads = [
        pltpu.make_async_copy(image_ref.at[pl.ds(pl.multiple_of(f * 128, 128), 128)], feat_i.at[0], local_sems.at[0]),
        pltpu.make_async_copy(text_ref, feat_t.at[0], local_sems.at[1]),
        pltpu.make_async_copy(w_image_ref, w_i.at[pl.ds(fw, slice_rows)], local_sems.at[2]),
        pltpu.make_async_copy(w_text_ref, w_t.at[pl.ds(fw, slice_rows)], local_sems.at[3]),
        pltpu.make_async_copy(
            image_ref.at[pl.ds(pl.multiple_of((zh * 2 + 1 - c) * 128, 128), 128)], peer_i.at[0], local_sems.at[4]
        ),
    ]
    for copy in loads:
        copy.start()
    barrier = pltpu.get_barrier_semaphore()
    for device in partners:
        pl.semaphore_signal(barrier, inc=1, device_id=device, device_id_type=MESH)
    pl.semaphore_wait(barrier, len(partners))
    for copy in loads:
        copy.wait()

    links = Links(send_sems, recv_sems)
    send = links.send

    def part_slots(ref, p):
        def slots(k, part):
            if part is None:
                return ref.at[PLACE[k, p]]
            return ref.at[PLACE[k, p], pl.ds(part * 64, 64)]
        return slots

    g_i = [RingGather(links, part_slots(feat_i, p), y_ring[1], y_ring[3]) for p in range(2)]
    g_t = [RingGather(links, part_slots(feat_t, p), x_ring[1], x_ring[3]) for p in range(2)]

    half = slice_rows // 2
    piece = half // 3
    fp = (1 - zh) * 2 + c

    def w_send(j, owner, which, device):
        w = (w_t, w_i)[j // 3]
        rows = pl.ds(pl.multiple_of(owner * slice_rows + which * half + (j % 3) * piece, 16), piece)
        return send(w.at[rows], w.at[rows], device)

    zx_t = send(feat_t.at[0], feat_t.at[1], z_part)
    zx_i = send(feat_i.at[0], feat_i.at[1], z_side)
    g_t[0].start()
    g_i[0].start()
    AHEAD = 3
    direct, side, core, last = [w_send(0, f, 1 - zl, z_part)], [], [], []
    w_pair = [send(w.at[pl.ds(fw, slice_rows)], w.at[pl.ds(fw, slice_rows)], other) for w in (w_t, w_i)]
    peers = [send(feat_t.at[0], peer_t.at[0], other)]

    def zero(i, carry):
        acc_t[pl.ds(pl.multiple_of(i * 128, 128), 128)] = jnp.zeros((128, E), F32)
        acc_i[pl.ds(pl.multiple_of(i * 64, 64), 64)] = jnp.zeros((64, E), F32)
        return carry

    lax.fori_loop(0, 16, zero, 0)
    temper = jnp.exp(jnp.full((8, 128), scale_ref[0], F32))
    t1 = temper[0:1, 0:1]
    offset = bias_ref[0]

    zx_t.wait_recv()
    direct += [w_send(j, f, 1 - zl, z_part) for j in range(1, AHEAD)]
    g_t[1].start()
    zx_i.wait_recv()
    g_i[1].start()
    g_t[0].forward()
    g_i[0].forward()

    def head_piece(j):
        direct[j].wait_recv()
        if j + AHEAD < 6:
            direct.append(w_send(j + AHEAD, f, 1 - zl, z_part))
        side.append(w_send(j, fp, zl, z_side))
        core.append(w_send(j, fp, zl, other))
        if j >= 1:
            side[j - 1].wait_recv()
            last.append(w_send(j - 1, fp, 1 - zl, other))

    def project(feat, w, places):
        rows = feat[places[0] : places[0] + 2].reshape(256, feat.shape[2])
        p = jnp.dot(rows, w[...], preferred_element_type=F32)
        inv = lax.rsqrt(jnp.sum(p * p, axis=-1, keepdims=True) + 1e-06)
        if places[0] == 0:
            proj[0 if w is w_i else 1] = p[0:128]
        emb = (p * inv).astype(BF)
        for at, place in enumerate(places):
            value = emb[at * 128 : at * 128 + 128]
            if w is w_i:
                emb_i[place * 128 : place * 128 + 128] = value
            else:
                emb_t[place * 256 : place * 256 + 128] = value
                emb_copies.append(
                    send(emb_t.at[pl.ds(place * 256, 128)], emb_t.at[pl.ds(place * 256 + 128, 128)], other)
                )

    emb_copies = []
    for j in range(4):
        head_piece(j)
    for copy in w_pair[0:1] + core[0:3] + last[0:3]:
        copy.wait_recv()
    project(feat_t, w_t, (2, 3))
    g_t[1].forward()
    g_i[1].forward()
    head_piece(4)
    g_t[0].finish()
    project(feat_t, w_t, (0, 1))
    head_piece(5)
    project(feat_t, w_t, (4, 5))
    g_t[1].finish()
    project(feat_t, w_t, (6, 7))
    side[5].wait_recv()
    last.append(w_send(5, fp, 1 - zl, other))
    peers.append(send(feat_t.at[1], peer_t.at[1], other))
    zpeer = send(feat_i.at[0], peer_i.at[1], z_part)
    for copy in w_pair[1:2] + core[3:6] + last[3:6]:
        copy.wait_recv()
    project(feat_i, w_i, (2, 3))
    project(feat_i, w_i, (0, 1))
    project(feat_i, w_i, (4, 5))
    g_i[0].finish()
    g_i[1].finish()
    project(feat_i, w_i, (6, 7))
    for copy in emb_copies:
        copy.wait_recv()
    zpeer.wait_recv()
    peers.append(send(peer_i.at[1], peer_i.at[2], other))
    for copy in peers[0:2]:
        copy.wait_recv()

    k1 = t1 * LOG2E
    k0 = offset * LOG2E

    def fold(v):
        v = jnp.sum(v.reshape(v.shape[0] // 8, 8, v.shape[1]), axis=0)
        return functools.reduce(jnp.add, [v[:, i : i + 512] for i in range(0, v.shape[1], 512)])

    def tile(ki, t0, nt, carry):
        s_loss, s_cos, s_sig = carry
        rows_i = pl.ds(ki * 256 if isinstance(ki, int) else pl.multiple_of(ki * 256, 256), 256)
        rows_t = pl.ds(t0, nt)
        a, b = emb_i[rows_i], emb_t[rows_t]
        cosines = lax.dot_general(a, b, LAST, preferred_element_type=F32)
        e = jnp.exp2(cosines * k1 + k0)
        s = 1.0 + e
        sig = e * pl.reciprocal(s, approx=False)
        low = sig.astype(BF)
        s_sig = s_sig + fold(sig)
        s_cos = s_cos + fold(sig * cosines)
        prod = (s[0:64] * s[64:128]) * (s[128:192] * s[192:256])
        s_loss = s_loss + fold(jnp.log(prod))
        acc_i[rows_i] += jnp.dot(low, b, preferred_element_type=F32)
        acc_t[rows_t] += lax.dot_general(low, a, FIRST, preferred_element_type=F32)
        return s_loss, s_cos, s_sig

    def get_i(p):
        return lambda k, part: acc_i[pl.ds(PLACE[k, p] * 128 + part * 64, 64)]

    def get_t(p):
        def get(k, part):
            at = PLACE[k, p]
            return acc_t[pl.ds(at * 256 + part * 64, 64)] + cross[pl.ds(at * 128 + part * 64, 64)]
        return get

    cuts = (64, 64)
    r_i = [
        RingSum(links, get_i(p), stage_i.at[p], far_r.at[p], near_r.at[p], cuts, y_ring[1], y_ring[3])
        for p in range(2)
    ]
    r_t = [
        RingSum(links, get_t(p), stage_t.at[p], far_r.at[2 + p], near_r.at[2 + p], cuts, x_ring[1], x_ring[3])
        for p in range(2)
    ]

    def cross_send(*places):
        return [
            send(acc_t.at[pl.ds(at * 256 + 128, 128)], cross.at[pl.ds(at * 128, 128)], other) for at in places
        ]

    def came(copies):
        for copy in copies:
            copy.wait_recv()

    zeros = jnp.zeros((8, 512), F32)
    sums = (zeros, zeros, zeros)
    sums = lax.fori_loop(0, 4, lambda i, v: tile(i, 1536, 512, v), sums)
    crossed = cross_send(6, 7)
    sums = tile(3, 0, 1536, sums)
    r_i[1].start_far()
    r_i[0].start_far()
    came(crossed)
    r_t[1].start_far()
    r_t[0].start_far()
    sums = lax.fori_loop(0, 3, lambda i, v: tile(i, 1024, 512, v), sums)
    crossed = cross_send(4, 5)
    sums = tile(2, 0, 1024, sums)
    r_i[1].start_left()
    r_i[1].start_right()
    came(crossed)
    r_t[1].start_left()
    r_t[1].start_right()
    r_i[1].forward()
    r_t[1].forward()
    sums = lax.fori_loop(0, 2, lambda i, v: tile(i, 512, 512, v), sums)
    crossed = cross_send(2, 3)
    sums = tile(1, 0, 512, sums)
    r_i[0].start_left()
    r_i[0].start_right()
    came(crossed)
    r_t[0].start_left()
    r_t[0].start_right()
    r_i[0].forward()
    r_t[0].forward()
    s_loss, s_cos, s_sig = tile(0, 0, 512, sums)
    crossed = cross_send(0, 1)
    came(crossed)
    z_copies = []
    for n, r, device in ((0, r_i, z_side), (1, r_t, z_part)):
        r[1].wait()
        for part in range(2):
            zsend[n, pl.ds(part * 64, 64)] = r[1].total(part).astype(BF)
        z_copies.append(send(zsend.at[n], zrecv.at[n], device))

    own_i = emb_i[0:128].astype(F32)
    own_t = emb_t[0:128].astype(F32)
    cos_d = jnp.sum(own_i * own_t, axis=-1, keepdims=True)
    l_d = cos_d * t1 + offset
    e_d = jnp.exp2(cos_d * k1 + k0)
    r_d = 1.0 / (1.0 + e_d)
    fix = -(r_d.astype(BF).astype(F32) + (e_d * r_d).astype(BF).astype(F32))

    def lanes(v):
        v = jnp.sum(v, axis=0, keepdims=True)
        return (v[:, 0:128] + v[:, 128:256]) + (v[:, 256:384] + v[:, 384:512])

    first_lane = lax.broadcasted_iota(jnp.int32, (1, 128), 1) == 0

    def less(v, total):
        return v - jnp.where(first_lane, total, 0.0)

    stat[...] = jnp.concatenate(
        [
            less(lanes(s_loss), jnp.sum(l_d)),
            less(lanes(s_cos), jnp.sum(cos_d)),
            less(lanes(s_sig), 128.0),
            jnp.zeros((5, 128), F32),
        ],
        axis=0,
    )

    st_c[c] = stat[...]
    st_copies = [send(stat, st_c.at[c], other)]
    def stat_sum(ref, count):
        v = ref[0]
        for k in range(1, count):
            v = v + ref[k]
        return v

    st_copies[0].wait_recv()
    stat_c = stat_sum(st_c, 2)
    st_x[x] = stat_c
    st_cx = [send(st_x.at[x], st_x.at[x], device) for device in x_ring[1:]]

    core_copies, part_copies = [], []
    gain = t1 * (1.0 / total_rows)
    for n, r in ((0, r_i[0]), (1, r_t[0])):
        r.wait()
        z_copies[n].wait_recv()
        partner_emb = own_t if n == 0 else own_i
        for part in range(2):
            rows = pl.ds(part * 64, 64)
            cut = slice(part * 64, part * 64 + 64)
            g = r.total(part) + zrecv[n, rows].astype(F32) + fix[cut] * partner_emb[cut]
            g = g * gain
            p = proj[n, rows]
            inv = lax.rsqrt(jnp.sum(p * p, axis=-1, keepdims=True) + 1e-06)
            unit = p * inv
            inner = jnp.sum(unit * g, axis=-1, keepdims=True)
            pg[n, 0, rows] = (inv * (g - unit * inner)).astype(BF)
        part_copies.append(send(pg.at[n, 0], pg.at[n, 2], z_part))
        core_copies.append(send(pg.at[n, 0], pg.at[n, 1], other))

    peers[2].wait_recv()
    rings = ((y_ring, y, x_ring, x), (x_ring, x, y_ring, y))
    bases = (0, 1160)
    last_copies = []
    for n in range(2):
        part_copies[n].wait_recv()
        last_copies.append(send(pg.at[n, 2], pg.at[n, 3], other))
    links.flush()
    for n in range(2):
        core_copies[n].wait_recv()
        last_copies[n].wait_recv()
    lhs = (
        jnp.concatenate([feat_i[0], peer_i[0], peer_i[1], peer_i[2]], axis=0),
        jnp.concatenate([feat_t[0], peer_t[0], feat_t[1], peer_t[1]], axis=0),
    )
    puts = []

    def steps(n, h):
        ring, r1, ring_2, r2 = rings[n]
        cols = pl.ds((0, 640)[h], (640, 512)[h])
        base = bases[n]
        rhs = pg[n, :, :, cols].reshape(512, cols.size)
        for q in range(3):
            acc_t[pl.ds(base + q * 384, 384), cols] = lax.dot_general(
                lhs[n][:, q * 384 : (q + 1) * 384], rhs, FIRST, preferred_element_type=F32
            )

        def get_m(k, part):
            first = base + f * slice_rows + ((r1 + k) % 4) * 72 + part * 48
            return acc_t[pl.ds(pl.multiple_of(first, 8), 48 - part * 16), cols]

        s = RingSum(
            links, get_m, stage_i.at[n, :, :, :, cols], far_p.at[n, :, :, cols], near_p.at[n, :, :, :, cols],
            (48, 32), ring[1], ring[3],
        )
        s.start()
        yield
        s.forward()
        yield
        s.wait()
        acc_p2[n, 0:48, cols] = s.total(0)
        acc_p2[n, 48:72, cols] = s.total(1)[0:24]
        acc_p2[n, 72:96, cols] = jnp.zeros((24, cols.size), F32)

        def get_2(k, part):
            first = ((r2 + k) % 4) * 24 + part * 16
            return acc_p2[n, pl.ds(pl.multiple_of(first, 8), 16 - part * 8), cols]

        s = RingSum(
            links, get_2, stage_p2.at[n, :, :, :, cols], far_p2.at[n, :, :, cols], near_p2.at[n, :, :, :, cols],
            (16, 8), ring_2[1], ring_2[3],
        )
        s.start()
        yield
        s.forward()
        yield
        s.wait()
        for part in range(2):
            z2s[n, pl.ds(part * 16, 16 - part * 8), cols] = s.total(part)
        copy = send(z2s.at[n, :, cols], z2.at[n, :, cols], z_side)
        yield
        copy.wait_recv()
        ag1[n, 0, :, cols] = z2s[n, :, cols] + z2[n, :, cols]

        def slots1(k, part):
            if part is None:
                return ag1.at[n, k, :, cols]
            return ag1.at[n, k, pl.ds(part * 16, 16 - part * 8), cols]

        g = RingGather(links, slots1, ring_2[1], ring_2[3])
        g.start()
        yield
        g.forward()
        yield
        g.finish()
        for k in range(4):
            ag2[n, 0, pl.ds(pl.multiple_of(((r2 + k) % 4) * 24, 8), 24), cols] = ag1[n, k, :, cols]

        def slots2(k, part):
            if part is None:
                return ag2.at[n, k, pl.ds(0, 72), cols]
            return ag2.at[n, k, pl.ds(part * 40, 40 - part * 8), cols]

        def put(k):
            out = (out_image, out_text)[n]
            copy = pltpu.make_async_copy(
                ag2.at[n, k, pl.ds(0, 72), cols],
                out.at[pl.ds(pl.multiple_of(((r1 + k) % 4) * 72, 8), 72), cols],
                local_sems.at[5 + (n * 2 + h) * 4 + k],
            )
            copy.start()
            puts.append(copy)

        g = RingGather(links, slots2, ring[1], ring[3])
        g.start()
        put(0)
        yield
        g.forward()
        put(1)
        put(3)
        yield
        g.finish()
        put(2)
        yield

    def share(ref, at, came_from, devices):
        ref[at] = came_from
        return [send(ref.at[at], ref.at[at], device) for device in devices]

    STEPS, SKEW = 10, 0
    chains = [(h * SKEW, steps(n, h)) for h in range(2) for n in range(2)]
    for t in range(STEPS + SKEW):
        for late, chain in chains:
            if 0 <= t - late < STEPS:
                next(chain)
        if t == 0:
            came(st_cx)
            st_cy = share(st_y, y, stat_sum(st_x, 4), y_ring[1:])
        if t == 3:
            came(st_cy)
            st_cz = share(st_z, z, stat_sum(st_y, 4), (z_side, z_part, z_diag))
        if t == 6:
            came(st_cz)
            stat_z = stat_sum(st_z, 4)
            out_loss[0] = jnp.sum(stat_z[0:1]) * (1.0 / total_rows / total_rows)
            out_scale[0] = jnp.sum(stat_z[1:2] * temper[0:1]) * (1.0 / total_rows)
            out_bias[0] = jnp.sum(stat_z[2:3]) * (1.0 / total_rows)
    for copy in puts:
        copy.wait()
    links.flush()


def solution(mesh):
    def body(image_feats, text_feats, w_image, w_text, logit_scale, logit_bias):
        width = w_image.shape[1]
        total = image_feats.shape[0] * mesh.shape["dp"]
        E = width
        hbm = pl.BlockSpec(memory_space=pl.ANY)
        smem = pl.BlockSpec(memory_space=pltpu.SMEM)
        V = pltpu.VMEM
        one = jax.ShapeDtypeStruct((1,), F32)
        outs = pl.pallas_call(
            functools.partial(kernel, width, total),
            out_shape=(
                jax.ShapeDtypeStruct(w_image.shape, F32),
                jax.ShapeDtypeStruct(w_text.shape, F32),
                one, one, one,
            ),
            in_specs=[hbm] * 4 + [smem] * 2,
            out_specs=(hbm, hbm, smem, smem, smem),
            scratch_shapes=[
                V((8, 128, E), BF),
                V((8, 128, E), BF),
                V((3, 128, E), BF),
                V((2, 128, E), BF),
                V((1152, E), BF),
                V((1152, E), BF),
                V((1024, E), BF),
                V((2048, E), BF),
                V((1024, E), F32),
                V((2328, E), F32),
                V((1024, E), F32),
                V((2, 3, 2, 64, E), BF),
                V((2, 3, 2, 64, E), BF),
                V((4, 2, 64, E), BF),
                V((4, 2, 2, 64, E), BF),
                V((2, 128, E), BF),
                V((2, 128, E), BF),
                V((2, 128, E), F32),
                V((2, 4, 128, E), BF),
                V((8, 128), F32),
                V((2, 8, 128), F32),
                V((4, 8, 128), F32),
                V((4, 8, 128), F32),
                V((4, 8, 128), F32),
                V((2, 2, 48, E), BF),
                V((2, 2, 2, 48, E), BF),
                V((2, 96, E), F32),
                V((2, 3, 2, 16, E), F32),
                V((2, 2, 16, E), F32),
                V((2, 2, 2, 16, E), F32),
                V((2, 24, E), F32),
                V((2, 24, E), F32),
                V((2, 4, 24, E), F32),
                V((2, 4, 96, E), F32),
                pltpu.SemaphoreType.DMA((200,)),
                pltpu.SemaphoreType.DMA((200,)),
                pltpu.SemaphoreType.DMA((24,)),
            ],
            compiler_params=pltpu.CompilerParams(
                collective_id=0, has_side_effects=True, vmem_limit_bytes=63 * 1024 * 1024
            ),
            cost_estimate=pl.CostEstimate(flops=16_000_000_000, bytes_accessed=20_000_000, transcendentals=6_000_000),
        )(image_feats, text_feats, w_image, w_text, logit_scale, logit_bias)
        g_image, g_text, loss, g_scale, g_bias = outs
        return (loss, g_image, g_text, g_scale, g_bias)

    placed = (P("dp", None), P(("dp", "fsdp"), None), P("fsdp", None), P("fsdp", None), P(), P())
    return jax.shard_map(
        body,
        mesh=mesh,
        in_specs=placed,
        out_specs=(P(), P("fsdp", None), P("fsdp", None), P(), P()),
        check_vma=False,
    )
```
